32 devices in a mesh: parts: 2 (over x), space: 16 (over z, y, core).
Axes of the slice: x: 2, y: 2, z: 4, core: 2. Of those that a mesh axis runs over, the one named last changes fastest.
Arguments:
- coefficients: bfloat16 [64, 4096], P('parts'), parts along dimension 0, may hold values from -6 to 6
- kl_modes: bfloat16 [8192, 2048], P('parts', 'space'), parts along dimension 0, may hold values from -0.09375 to 0.09375
- green: bfloat16 [4096, 256, 128], P(('parts', 'space')), parts along dimension 0, may hold values from -0.1875 to 0.1875
- sub_index: int32 [4096], P('parts'), parts along dimension 0, may hold values from 0 to 2047, each once
- kernel: float32 [33, 33], replicated, may hold values from 0.2 to 5
- wet_mask: int32 [512, 128], P(('parts', 'space')), parts along dimension 0, may hold values 0 or 1
Outputs:
- surface: float32 [64, 256, 128], P('parts', 'space'), parts along dimension 0
The draws below stay inside these ranges and needn't reach their ends.
There are 2 independent parts, one for each index of `parts`. The reference program is written for one: setup_inputs(seed, part) draws one part's arguments, and reference() takes and returns one part's arrays. A program takes and returns all parts, laid end to end along the dimension named above; an argument that names none is the same for every part. Nothing has to cross between parts.
Inputs may be any that keep to these rules, and one draw needn't show every extreme that they name: `sub_index`: each subfault appears once.
All inputs are finite; a program needn't handle non-finite values. No bound on the sum of `wet_mask` on one device may be relied on, other than what follows from the above.
Results may differ from the reference program's by a relative error of at most 0.005.
Values may be sent and summed in bfloat16 or wider, within the bound.
A program may use at most 128 MiB of HBM per device.

```python
import math
import jax
import jax.numpy as jnp
from jax import lax

R = 32
M = 4096
S = 2048
CX = 16
NY = 128
HALF = 16
TAPS = 33
NX = 256


def set_ends(drawn, own_key, smallest, top_value):
    place = [jax.random.randint(jax.random.fold_in(own_key, axis), (), 0, length) for axis, length in enumerate(drawn.shape)]
    longest = drawn.shape.index(max(drawn.shape))
    next_to = place[:longest] + [(place[longest] + 1) % drawn.shape[longest]] + place[longest + 1:]
    return drawn.at[tuple(place)].set(smallest).at[tuple(next_to)].set(top_value)


def spiked(result, rng, source, target, blocks, factor):
    owner, partner = [(jnp.arange(result.shape[dim]) // (result.shape[dim] // blocks)).reshape([-1 if axis == dim else 1 for axis in range(result.ndim)]) for dim in (source, target)]
    chosen = jax.random.permutation(rng, blocks)[partner]
    strong = (owner == chosen) | (owner == (partner + blocks // 2) % blocks)
    return jnp.where(strong, factor * result, result)


def block_levels(stream_key, shape, split, least, largest):
    level, own = 1.0, jax.random.fold_in(stream_key, 6)
    for dim, shards_of in split:
        steps = jnp.exp(jax.random.uniform(jax.random.fold_in(own, dim), (shards_of,), jnp.float32, least / len(split), largest / len(split)))
        level = level * jnp.repeat(steps, shape[dim] // shards_of).reshape([-1 if axis == dim else 1 for axis in range(len(shape))])
    return level


def bell_draw(rng, dims, scale, most, shards=(), kind=jnp.bfloat16):
    values = scale * jax.random.normal(rng, dims, jnp.float32)
    if shards:
        values = values * block_levels(rng, dims, shards, -0.22, 0.18)
    return jnp.clip(values, -most, most).astype(kind)


def bell_draw_with(rng, extent, spread, bound, shards, heavy, kind=jnp.bfloat16):
    entries = spread * jax.random.normal(rng, extent, jnp.float32)
    if shards:
        entries = entries * block_levels(rng, extent, shards, -0.22, 0.18)
    return jnp.clip(spiked(entries, jax.random.fold_in(rng, 3), *heavy), -bound, bound).astype(kind)


def setup_inputs(seed: int = 0, part: int = 0) -> dict:
    splits = jax.random.split(jax.random.key(seed), 7)
    part_splits = jax.random.split(jax.random.fold_in(splits[6], part), 7)
    coefficients = bell_draw(part_splits[0], (R, M), 1.0, 6.0)
    kl_modes = bell_draw(part_splits[1], (M, S), M ** -0.5, 0.09375, ((1, 16),))
    green = bell_draw_with(part_splits[2], (S, NX, NY), S ** -0.5, 0.1875, ((0, 16),), (0, 1, 16, 2.0))
    sub_index = jax.random.permutation(part_splits[3], S).astype(jnp.int32)
    kernel = jnp.clip(jnp.exp(jax.random.uniform(splits[4], (TAPS, TAPS), jnp.float32, math.log(0.2), math.log(5.0))), 0.2, 5.0)
    wet_mask = set_ends((jax.random.randint(part_splits[5], (NX, NY), 0, 4) < 3).astype(jnp.int32), jax.random.fold_in(part_splits[5], 1), 0, 1)
    return dict(coefficients=coefficients, kl_modes=kl_modes, green=green, sub_index=sub_index, kernel=kernel, wet_mask=wet_mask)


def make_bands(weights, width):
    half = weights.shape[1] // 2
    source = lax.broadcasted_iota(jnp.int32, (width, width), 0)
    target = lax.broadcasted_iota(jnp.int32, (width, width), 1)
    offset = source - target + half
    inside = (offset >= 0) & (offset <= 2 * half)
    picked = jnp.take(weights, jnp.clip(offset, 0, 2 * half).astype(jnp.int32), axis=1)
    return jnp.where(inside[None], picked, jnp.zeros_like(picked))


def reference(coefficients, kl_modes, green, sub_index, kernel, wet_mask):
    field = jnp.dot(coefficients, kl_modes, preferred_element_type=jnp.float32)
    slip = jnp.exp(0.5 * field).astype(jnp.bfloat16)
    slip_rows = jnp.take(slip, sub_index, axis=1).astype(jnp.float32)

    def block(index):
        tile = lax.dynamic_slice_in_dim(green, index * CX, CX, 1).astype(jnp.float32)
        return jnp.dot(slip_rows, tile.reshape(S, CX * NY), precision=lax.Precision.HIGHEST)

    blocks = lax.map(block, jnp.arange(NX // CX, dtype=jnp.int32))
    uplift = blocks.reshape(NX // CX, R, CX, NY).transpose(1, 0, 2, 3).reshape(R, NX, NY)
    seafloor = uplift.astype(jnp.bfloat16).astype(jnp.float32)
    weights = (kernel / jnp.sum(kernel)).astype(jnp.bfloat16).astype(jnp.float32)
    bands = make_bands(weights, NY)
    padded = jnp.pad(seafloor, ((0, 0), (HALF, HALF), (0, 0)))
    smooth = jnp.zeros((R * NX, NY), jnp.float32)
    for shift_row in range(TAPS):
        rows = padded[:, shift_row:shift_row + NX, :].reshape(R * NX, NY)
        smooth = smooth + jnp.dot(rows, bands[shift_row], precision=lax.Precision.HIGHEST)
    return smooth.reshape(R, NX, NY) * wet_mask.astype(jnp.float32)[None]
```

```python
import functools
import jax
import jax.numpy as jnp
from jax import lax
from jax.experimental import pallas as pl
from jax.experimental.pallas import tpu as pltpu
from jax.sharding import PartitionSpec as P

SPAN = 8


def remote(source, target, send, receive, peer):
    return pltpu.make_async_remote_copy(
        src_ref=source,
        dst_ref=target,
        send_sem=send,
        recv_sem=receive,
        device_id={"space": peer},
        device_id_type=pl.DeviceIdType.MESH,
    )


def source_kernel(
    n,
    coef_hbm, modes_hbm, green_hbm, index_ref, taps_ref, wet_ref,
    out_ref,
    coef, modes, green, slots, hots, spread, lhs, bands, rows_of,
    send_c, recv_c, keep, send_y, recv_y, send_z, recv_z, padded,
    load_sem, green_sem, slip_send, slip_recv,
    c_send, c_recv, y_send, y_recv, z_send, z_recv, halo_send, halo_recv,
):
    f32, bf16 = jnp.float32, jnp.bfloat16
    me = lax.axis_index("space")
    planes = n // 4
    z, y, c = me // 4, (me // 2) % 2, me % 2
    core_peer = me + 1 - 2 * c
    y_peer = me + 2 - 4 * y
    realizations, per = slots.shape[1], slots.shape[2]
    group, tile, width = green.shape[2], green.shape[3], green.shape[4]
    rows = tile * realizations
    taps = taps_ref.shape[0]
    half = taps // 2
    edge = half * realizations

    load_coef = pltpu.make_async_copy(coef_hbm, coef, load_sem.at[0])
    load_modes = pltpu.make_async_copy(modes_hbm, modes, load_sem.at[1])
    load_coef.start()
    load_modes.start()

    def plane_of(step):
        return lax.rem(z + 1 + step, planes)

    def green_copy(step, across, beside):
        block = plane_of(step) * 4 + ((y + beside) % 2) * 2 + (c + across) % 2
        return pltpu.make_async_copy(
            green_hbm.at[:, pl.ds(pl.multiple_of(block * tile, tile), tile), :],
            green.at[step, across * 2 + beside],
            green_sem.at[step, across * 2 + beside],
        )

    barrier = pltpu.get_barrier_semaphore()
    for k in range(1, n):
        pl.semaphore_signal(
            barrier, inc=1, device_id={"space": lax.rem(me + k, n)},
            device_id_type=pl.DeviceIdType.MESH,
        )
    for step in range(planes):
        for across in (1, 0):
            for beside in (0, 1):
                green_copy(step, across, beside).start()

    load_coef.wait()
    load_modes.wait()
    field = jnp.dot(coef[...], modes[...], preferred_element_type=f32)
    slots[me] = jnp.exp(0.5 * field).astype(bf16)
    pl.semaphore_wait(barrier, n - 1)

    def slip_copy(k):
        return remote(
            slots.at[me], slots.at[me], slip_send.at[k], slip_recv.at[k], lax.rem(me + k, n)
        )

    for k in range(1, n):
        slip_copy(k).start()

    wanted = index_ref[pl.ds(me, 1), :]
    first = lax.broadcasted_iota(jnp.int32, (per, group), 0)
    for d in range(n):
        hots[d] = (first + d * per == wanted).astype(f32).astype(bf16)
    column = lax.broadcasted_iota(jnp.int32, (group, group * tile), 1)
    owner = lax.broadcasted_iota(jnp.int32, (group, group * tile), 0)
    spread[...] = (column // tile == owner).astype(f32).astype(bf16)
    raw = taps_ref[...]
    weights = (raw / jnp.sum(raw)).astype(bf16)
    tap = lax.broadcasted_iota(jnp.int32, (taps, width), 0)
    lane = lax.broadcasted_iota(jnp.int32, (taps, width), 1)
    place = ((half - tap + width) % width == lane).astype(f32).astype(bf16)
    rows_of[...] = jnp.dot(weights, place, preferred_element_type=f32)
    source = lax.broadcasted_iota(jnp.int32, (width, width), 0)
    target = lax.broadcasted_iota(jnp.int32, (width, width), 1)
    inside = jnp.abs(source - target) <= half
    for a in range(taps):
        line = jnp.broadcast_to(rows_of[a : a + 1, :], (width, width))
        line = pltpu.roll(line, 0, 1, stride=1, stride_axis=0)
        bands[a * width : (a + 1) * width, :] = jnp.where(inside, line, 0.0).astype(bf16)

    for k in range(1, n):
        slip_copy(k).wait_recv()
    picked = jnp.zeros((realizations, group), f32)
    for d in range(n):
        picked += jnp.dot(slots[d], hots[d], preferred_element_type=f32)
    repeated = jnp.dot(picked.astype(bf16), spread[...], preferred_element_type=f32)
    inner = lax.broadcasted_iota(jnp.int32, repeated.shape, 1) % tile
    for x in range(tile):
        lhs[x * realizations : (x + 1) * realizations, :] = jnp.where(
            inner == x, repeated, 0.0
        ).astype(bf16)

    def c_copy(step):
        return remote(
            send_c.at[step], recv_c.at[step], c_send.at[step], c_recv.at[step], core_peer
        )

    def y_copy(step):
        return remote(send_y.at[step], recv_y.at[step], y_send.at[step], y_recv.at[step], y_peer)

    def z_copy(step):
        return remote(
            send_z.at[step], recv_z.at[step], z_send.at[step], z_recv.at[step],
            plane_of(step) * 4 + y * 2 + c,
        )

    def multiply(step, across):
        sides = []
        for beside in (0, 1):
            green_copy(step, across, beside).wait()
            sides.append(green[step, across * 2 + beside].reshape(group * tile, width))
        return jnp.dot(lhs[...], jnp.concatenate(sides, axis=1), preferred_element_type=f32)

    def stage(t, carry):
        @pl.when(t < planes)
        def _():
            result = multiply(t, 1)
            for beside in (0, 1):
                send_c[t, beside] = result[:, beside * width : (beside + 1) * width].astype(bf16)
            c_copy(t).start()
            result = multiply(t, 0)
            for beside in (0, 1):
                keep[t, beside] = result[:, beside * width : (beside + 1) * width]

        @pl.when((t >= 1) & (t <= planes))
        def _():
            step = t - 1
            c_copy(step).wait_recv()
            send_y[step] = (keep[step, 1] + recv_c[step, 1].astype(f32)).astype(bf16)
            y_copy(step).start()
            keep[step, 0] = keep[step, 0] + recv_c[step, 0].astype(f32)

        @pl.when((t >= 2) & (t <= planes))
        def _():
            step = t - 2
            y_copy(step).wait_recv()
            send_z[step] = (keep[step, 0] + recv_y[step].astype(f32)).astype(bf16)
            z_copy(step).start()

        return carry

    lax.fori_loop(0, planes + 1, stage, 0)
    last = planes - 1
    y_copy(last).wait_recv()
    total = keep[last, 0] + recv_y[last].astype(f32)
    for step in range(last):
        z_copy(step).wait_recv()
        total += recv_z[step].astype(f32)
    padded[edge : edge + rows, :] = total.astype(bf16)

    up = remote(
        padded.at[pl.ds(rows, edge)], padded.at[pl.ds(0, edge)],
        halo_send.at[0], halo_recv.at[0], lax.rem(me + 1, n),
    )
    down = remote(
        padded.at[pl.ds(edge, edge)], padded.at[pl.ds(edge + rows, edge)],
        halo_send.at[1], halo_recv.at[1], lax.rem(me + n - 1, n),
    )
    has_low, has_high = me > 0, me < n - 1
    pl.when(has_high)(lambda: up.start())
    pl.when(has_low)(lambda: down.start())

    @pl.when(me == 0)
    def _():
        padded[0:edge, :] = jnp.zeros((edge, width), bf16)

    @pl.when(me == n - 1)
    def _():
        padded[edge + rows :, :] = jnp.zeros((edge, width), bf16)

    pl.when(has_low)(lambda: up.wait_recv())
    pl.when(has_high)(lambda: down.wait_recv())

    smooth = None
    for begin in range(0, taps, SPAN):
        end = min(taps, begin + SPAN)
        windows = jnp.concatenate(
            [
                padded[a * realizations : a * realizations + rows, :]
                for a in range(begin, end)
            ],
            axis=1,
        )
        term = jnp.dot(
            windows, bands[begin * width : end * width, :], preferred_element_type=f32
        )
        smooth = term if smooth is None else smooth + term
    wet = wet_ref[...].astype(f32)
    for x in range(tile):
        out_ref[x] = smooth[x * realizations : (x + 1) * realizations, :] * wet[x : x + 1, :]

    for k in range(1, n):
        slip_copy(k).wait_send()
    for step in range(planes):
        c_copy(step).wait_send()
        y_copy(step).wait_send()
    for step in range(last):
        z_copy(step).wait_send()
    pl.when(has_high)(lambda: up.wait_send())
    pl.when(has_low)(lambda: down.wait_send())


def on_device(coefficients, kl_modes, green, sub_index, kernel, wet_mask):
    bf16, f32 = jnp.bfloat16, jnp.float32
    n = lax.axis_size("space")
    planes = n // 4
    realizations, modes = coefficients.shape
    per = kl_modes.shape[1]
    group, _, width = green.shape
    tile = wet_mask.shape[0]
    taps = kernel.shape[0]
    rows = tile * realizations
    edge = taps // 2 * realizations
    dma = pltpu.SemaphoreType.DMA
    vmem = pl.BlockSpec(memory_space=pltpu.VMEM)
    hbm = pl.BlockSpec(memory_space=pl.ANY)
    surface = pl.pallas_call(
        functools.partial(source_kernel, n),
        out_shape=jax.ShapeDtypeStruct((tile, realizations, width), f32),
        in_specs=[hbm, hbm, hbm, vmem, vmem, vmem],
        out_specs=vmem,
        scratch_shapes=[
            pltpu.VMEM((realizations, modes), bf16),
            pltpu.VMEM((modes, per), bf16),
            pltpu.VMEM((planes, 4, group, tile, width), bf16),
            pltpu.VMEM((n, realizations, per), bf16),
            pltpu.VMEM((n, per, group), bf16),
            pltpu.VMEM((group, group * tile), bf16),
            pltpu.VMEM((rows, group * tile), bf16),
            pltpu.VMEM((taps * width, width), bf16),
            pltpu.VMEM((taps, width), f32),
            pltpu.VMEM((planes, 2, rows, width), bf16),
            pltpu.VMEM((planes, 2, rows, width), bf16),
            pltpu.VMEM((planes, 2, rows, width), f32),
            pltpu.VMEM((planes, rows, width), bf16),
            pltpu.VMEM((planes, rows, width), bf16),
            pltpu.VMEM((planes, rows, width), bf16),
            pltpu.VMEM((planes, rows, width), bf16),
            pltpu.VMEM((rows + 2 * edge, width), bf16),
            dma((2,)),
            dma((planes, 4)),
            dma((n,)),
            dma((n,)),
            dma((planes,)),
            dma((planes,)),
            dma((planes,)),
            dma((planes,)),
            dma((planes,)),
            dma((planes,)),
            dma((2,)),
            dma((2,)),
        ],
        compiler_params=pltpu.CompilerParams(
            collective_id=0, has_side_effects=True, vmem_limit_bytes=56 * 2**20
        ),
    )(coefficients, kl_modes, green, sub_index.reshape(n, group), kernel, wet_mask)
    return surface.transpose(1, 0, 2)


def solution(mesh):
    placed = (
        P("parts", None),
        P("parts", "space"),
        P(("parts", "space"), None, None),
        P("parts"),
        P(),
        P(("parts", "space"), None),
    )
    return jax.shard_map(
        on_device, mesh=mesh, in_specs=placed, out_specs=P("parts", "space", None), check_vma=False
    )
```

```python
import functools
import jax
import jax.numpy as jnp
from jax import lax
from jax.experimental import pallas as pl
from jax.experimental.pallas import tpu as pltpu
from jax.sharding import PartitionSpec as P

SPAN = 8


def remote(source, target, send, receive, peer):
    return pltpu.make_async_remote_copy(
        src_ref=source,
        dst_ref=target,
        send_sem=send,
        recv_sem=receive,
        device_id={"space": peer},
        device_id_type=pl.DeviceIdType.MESH,
    )


def source_kernel(
    n,
    coef_hbm, modes_hbm, green_hbm, index_ref, taps_ref, wet_ref,
    out_ref,
    coef, modes, green, slots, hots, spread, lhs, bands, rows_of,
    send_c, recv_c, keep, send_y, recv_y, send_z, recv_z, padded,
    load_sem, green_sem, slip_send, slip_recv,
    c_send, c_recv, y_send, y_recv, z_send, z_recv, halo_send, halo_recv,
):
    f32, bf16 = jnp.float32, jnp.bfloat16
    me = lax.axis_index("space")
    planes = n // 4
    z, y, c = me // 4, (me // 2) % 2, me % 2
    core_peer = me + 1 - 2 * c
    y_peer = me + 2 - 4 * y
    q = me % 4
    realizations, per = slots.shape[2], slots.shape[3]
    group, tile, width = green.shape[2], green.shape[3], green.shape[4]
    rows = tile * realizations
    taps = taps_ref.shape[0]
    half = taps // 2
    edge = half * realizations

    load_coef = pltpu.make_async_copy(coef_hbm, coef, load_sem.at[0])
    load_modes = pltpu.make_async_copy(modes_hbm, modes, load_sem.at[1])
    load_coef.start()
    load_modes.start()

    middle = planes // 2

    def across_planes(offset):
        result, bit = 0, 1
        while bit < planes:
            result = result + ((z // bit + offset // bit) % 2) * bit
            bit *= 2
        return result

    def plane_of(step):
        early = jnp.where(step == middle - 1, 1, 2 * step + 3)
        late = jnp.where(step == planes - 1, 0, 2 * (step - middle) + 2)
        return across_planes(jnp.where(step < middle, early, late))

    def green_copy(step, across, beside):
        block = plane_of(step) * 4 + ((y + beside) % 2) * 2 + (c + across) % 2
        return pltpu.make_async_copy(
            green_hbm.at[:, pl.ds(pl.multiple_of(block * tile, tile), tile), :],
            green.at[step, across * 2 + beside],
            green_sem.at[step, across * 2 + beside],
        )

    barrier = pltpu.get_barrier_semaphore()
    for k in range(1, n):
        pl.semaphore_signal(
            barrier, inc=1, device_id={"space": lax.rem(me + k, n)},
            device_id_type=pl.DeviceIdType.MESH,
        )
    for step in range(planes):
        for across in (1, 0):
            for beside in (0, 1):
                green_copy(step, across, beside).start()

    load_coef.wait()
    load_modes.wait()
    field = jnp.dot(coef[...], modes[...], preferred_element_type=f32)
    slots[q, z] = jnp.exp(0.5 * field).astype(bf16)
    pl.semaphore_wait(barrier, n - 1)

    def line_copy(k):
        return remote(
            slots.at[q, z], slots.at[q, z], slip_send.at[k], slip_recv.at[k],
            lax.rem(z + k, planes) * 4 + q,
        )

    def plane_copy(k):
        return remote(
            slots.at[q], slots.at[q], slip_send.at[planes + k], slip_recv.at[planes + k],
            z * 4 + lax.rem(q + k, 4),
        )

    for k in range(1, planes):
        line_copy(k).start()

    wanted = index_ref[pl.ds(me, 1), :]
    first = lax.broadcasted_iota(jnp.int32, (per, group), 0)
    for d in range(n):
        hots[d % 4, d // 4] = (first + d * per == wanted).astype(f32).astype(bf16)
    for k in range(1, planes):
        line_copy(k).wait_recv()
    for k in range(1, 4):
        plane_copy(k).start()
    column = lax.broadcasted_iota(jnp.int32, (group, group * tile), 1)
    owner = lax.broadcasted_iota(jnp.int32, (group, group * tile), 0)
    spread[...] = (column // tile == owner).astype(f32).astype(bf16)
    raw = taps_ref[...]
    weights = (raw / jnp.sum(raw)).astype(bf16)
    tap = lax.broadcasted_iota(jnp.int32, (taps, width), 0)
    lane = lax.broadcasted_iota(jnp.int32, (taps, width), 1)
    place = ((half - tap + width) % width == lane).astype(f32).astype(bf16)
    rows_of[...] = jnp.dot(weights, place, preferred_element_type=f32)
    source = lax.broadcasted_iota(jnp.int32, (width, width), 0)
    target = lax.broadcasted_iota(jnp.int32, (width, width), 1)
    inside = jnp.abs(source - target) <= half
    for a in range(taps):
        line = jnp.broadcast_to(rows_of[a : a + 1, :], (width, width))
        line = pltpu.roll(line, 0, 1, stride=1, stride_axis=0)
        bands[a * width : (a + 1) * width, :] = jnp.where(inside, line, 0.0).astype(bf16)

    picked = jnp.zeros((realizations, group), f32)
    for k in range(4):
        if k:
            plane_copy(k).wait_recv()
        held = lax.rem(q + 4 - k, 4)
        for d in range(planes):
            picked += jnp.dot(slots[held, d], hots[held, d], preferred_element_type=f32)
    repeated = jnp.dot(picked.astype(bf16), spread[...], preferred_element_type=f32)
    inner = lax.broadcasted_iota(jnp.int32, repeated.shape, 1) % tile
    for x in range(tile):
        lhs[x * realizations : (x + 1) * realizations, :] = jnp.where(
            inner == x, repeated, 0.0
        ).astype(bf16)

    def c_copy(step):
        return remote(
            send_c.at[step], recv_c.at[step], c_send.at[step], c_recv.at[step], core_peer
        )

    def y_copy(step):
        return remote(send_y.at[step], recv_y.at[step], y_send.at[step], y_recv.at[step], y_peer)

    def z_copy(step):
        return remote(
            send_z.at[step], recv_z.at[step], z_send.at[step], z_recv.at[step],
            jnp.where(step < middle, across_planes(1), plane_of(step)) * 4 + q,
        )

    def multiply(step, across):
        sides = []
        for beside in (0, 1):
            green_copy(step, across, beside).wait()
            sides.append(green[step, across * 2 + beside].reshape(group * tile, width))
        return jnp.dot(lhs[...], jnp.concatenate(sides, axis=1), preferred_element_type=f32)

    def stage(t, carry):
        result = multiply(t, 1)
        for beside in (0, 1):
            send_c[t, beside] = result[:, beside * width : (beside + 1) * width].astype(bf16)
        c_copy(t).start()
        result = multiply(t, 0)
        for beside in (0, 1):
            keep[t, beside] = result[:, beside * width : (beside + 1) * width]

        c_copy(t).wait_recv()
        send_y[t] = (keep[t, 1] + recv_c[t, 1].astype(f32)).astype(bf16)
        y_copy(t).start()
        keep[t, 0] = keep[t, 0] + recv_c[t, 0].astype(f32)

        @pl.when(t >= 1)
        def _():
            step = t - 1
            y_copy(step).wait_recv()
            keep[step, 0] = keep[step, 0] + recv_y[step].astype(f32)

            @pl.when(step >= middle)
            def _():
                z_copy(step - middle).wait_recv()
                keep[step, 0] = keep[step, 0] + recv_z[step - middle].astype(f32)

            send_z[step] = keep[step, 0].astype(bf16)
            z_copy(step).start()

        return carry

    lax.fori_loop(0, planes, stage, 0)
    last = planes - 1
    y_copy(last).wait_recv()
    total = keep[last, 0] + recv_y[last].astype(f32)
    for step in range(middle - 1, last):
        z_copy(step).wait_recv()
        total += recv_z[step].astype(f32)
    padded[edge : edge + rows, :] = total.astype(bf16)

    up = remote(
        padded.at[pl.ds(rows, edge)], padded.at[pl.ds(0, edge)],
        halo_send.at[0], halo_recv.at[0], lax.rem(me + 1, n),
    )
    down = remote(
        padded.at[pl.ds(edge, edge)], padded.at[pl.ds(edge + rows, edge)],
        halo_send.at[1], halo_recv.at[1], lax.rem(me + n - 1, n),
    )
    has_low, has_high = me > 0, me < n - 1
    pl.when(has_high)(lambda: up.start())
    pl.when(has_low)(lambda: down.start())

    @pl.when(me == 0)
    def _():
        padded[0:edge, :] = jnp.zeros((edge, width), bf16)

    @pl.when(me == n - 1)
    def _():
        padded[edge + rows :, :] = jnp.zeros((edge, width), bf16)

    pl.when(has_low)(lambda: up.wait_recv())
    pl.when(has_high)(lambda: down.wait_recv())

    smooth = None
    for begin in range(0, taps, SPAN):
        end = min(taps, begin + SPAN)
        windows = jnp.concatenate(
            [
                padded[a * realizations : a * realizations + rows, :]
                for a in range(begin, end)
            ],
            axis=1,
        )
        term = jnp.dot(
            windows, bands[begin * width : end * width, :], preferred_element_type=f32
        )
        smooth = term if smooth is None else smooth + term
    wet = wet_ref[...].astype(f32)
    for x in range(tile):
        out_ref[x] = smooth[x * realizations : (x + 1) * realizations, :] * wet[x : x + 1, :]

    for k in range(1, planes):
        line_copy(k).wait_send()
    for k in range(1, 4):
        plane_copy(k).wait_send()
    for step in range(planes):
        c_copy(step).wait_send()
        y_copy(step).wait_send()
    for step in range(last):
        z_copy(step).wait_send()
    pl.when(has_high)(lambda: up.wait_send())
    pl.when(has_low)(lambda: down.wait_send())


def on_device(coefficients, kl_modes, green, sub_index, kernel, wet_mask):
    bf16, f32 = jnp.bfloat16, jnp.float32
    n = lax.axis_size("space")
    planes = n // 4
    realizations, modes = coefficients.shape
    per = kl_modes.shape[1]
    group, _, width = green.shape
    tile = wet_mask.shape[0]
    taps = kernel.shape[0]
    rows = tile * realizations
    edge = taps // 2 * realizations
    dma = pltpu.SemaphoreType.DMA
    vmem = pl.BlockSpec(memory_space=pltpu.VMEM)
    hbm = pl.BlockSpec(memory_space=pl.ANY)
    surface = pl.pallas_call(
        functools.partial(source_kernel, n),
        out_shape=jax.ShapeDtypeStruct((tile, realizations, width), f32),
        in_specs=[hbm, hbm, hbm, vmem, vmem, vmem],
        out_specs=vmem,
        scratch_shapes=[
            pltpu.VMEM((realizations, modes), bf16),
            pltpu.VMEM((modes, per), bf16),
            pltpu.VMEM((planes, 4, group, tile, width), bf16),
            pltpu.VMEM((4, planes, realizations, per), bf16),
            pltpu.VMEM((4, planes, per, group), bf16),
            pltpu.VMEM((group, group * tile), bf16),
            pltpu.VMEM((rows, group * tile), bf16),
            pltpu.VMEM((taps * width, width), bf16),
            pltpu.VMEM((taps, width), f32),
            pltpu.VMEM((planes, 2, rows, width), bf16),
            pltpu.VMEM((planes, 2, rows, width), bf16),
            pltpu.VMEM((planes, 2, rows, width), f32),
            pltpu.VMEM((planes, rows, width), bf16),
            pltpu.VMEM((planes, rows, width), bf16),
            pltpu.VMEM((planes, rows, width), bf16),
            pltpu.VMEM((planes, rows, width), bf16),
            pltpu.VMEM((rows + 2 * edge, width), bf16),
            dma((2,)),
            dma((planes, 4)),
            dma((planes + 4,)),
            dma((planes + 4,)),
            dma((planes,)),
            dma((planes,)),
            dma((planes,)),
            dma((planes,)),
            dma((planes,)),
            dma((planes,)),
            dma((2,)),
            dma((2,)),
        ],
        compiler_params=pltpu.CompilerParams(
            collective_id=0, has_side_effects=True, vmem_limit_bytes=56 * 2**20
        ),
    )(coefficients, kl_modes, green, sub_index.reshape(n, group), kernel, wet_mask)
    return surface.transpose(1, 0, 2)


def solution(mesh):
    placed = (
        P("parts", None),
        P("parts", "space"),
        P(("parts", "space"), None, None),
        P("parts"),
        P(),
        P(("parts", "space"), None),
    )
    return jax.shard_map(
        on_device, mesh=mesh, in_specs=placed, out_specs=P("parts", "space", None), check_vma=False
    )
```

```python
import functools
import jax
import jax.numpy as jnp
from jax import lax
from jax.experimental import pallas as pl
from jax.experimental.pallas import tpu as pltpu
from jax.sharding import PartitionSpec as P

SPAN = 8


def remote(source, target, send, receive, peer):
    return pltpu.make_async_remote_copy(
        src_ref=source,
        dst_ref=target,
        send_sem=send,
        recv_sem=receive,
        device_id={"space": peer},
        device_id_type=pl.DeviceIdType.MESH,
    )


def source_kernel(
    n,
    coef_hbm, modes_hbm, green_hbm, index_ref, taps_ref, wet_ref,
    out_ref,
    coef, modes, green, slots, hots, spread, lhs, bands, rows_of,
    send_c, recv_c, keep, send_y, recv_y, send_z, recv_z, padded,
    load_sem, green_sem, slip_send, slip_recv,
    c_send, c_recv, y_send, y_recv, z_send, z_recv, halo_send, halo_recv,
):
    f32, bf16 = jnp.float32, jnp.bfloat16
    me = lax.axis_index("space")
    planes = n // 4
    z, y, c = me // 4, (me // 2) % 2, me % 2
    core_peer = me + 1 - 2 * c
    y_peer = me + 2 - 4 * y
    q = me % 4
    realizations, per = slots.shape[2], slots.shape[3]
    group, tile, width = green.shape[2], green.shape[3], green.shape[4]
    rows = tile * realizations
    taps = taps_ref.shape[0]
    half = taps // 2
    edge = half * realizations

    load_coef = pltpu.make_async_copy(coef_hbm, coef, load_sem.at[0])
    load_modes = pltpu.make_async_copy(modes_hbm, modes, load_sem.at[1])
    load_coef.start()
    load_modes.start()

    def plane_of(step):
        middle = planes // 2
        ahead = jnp.where(step == 0, middle, jnp.where(step < middle, step, step + 1))
        return lax.rem(z + ahead, planes)

    def green_copy(step, across, beside):
        block = plane_of(step) * 4 + ((y + beside) % 2) * 2 + (c + across) % 2
        return pltpu.make_async_copy(
            green_hbm.at[:, pl.ds(pl.multiple_of(block * tile, tile), tile), :],
            green.at[step, across * 2 + beside],
            green_sem.at[step, across * 2 + beside],
        )

    barrier = pltpu.get_barrier_semaphore()
    for k in range(1, n):
        pl.semaphore_signal(
            barrier, inc=1, device_id={"space": lax.rem(me + k, n)},
            device_id_type=pl.DeviceIdType.MESH,
        )
    for step in range(planes):
        for across in (1, 0):
            for beside in (0, 1):
                green_copy(step, across, beside).start()

    load_coef.wait()
    load_modes.wait()
    field = jnp.dot(coef[...], modes[...], preferred_element_type=f32)
    slots[q, z] = jnp.exp(0.5 * field).astype(bf16)
    pl.semaphore_wait(barrier, n - 1)

    def line_copy(k):
        return remote(
            slots.at[q, z], slots.at[q, z], slip_send.at[k], slip_recv.at[k],
            lax.rem(z + k, planes) * 4 + q,
        )

    def plane_copy(k):
        return remote(
            slots.at[q], slots.at[q], slip_send.at[planes + k], slip_recv.at[planes + k],
            z * 4 + lax.rem(q + k, 4),
        )

    for k in range(1, planes):
        line_copy(k).start()

    wanted = index_ref[pl.ds(me, 1), :]
    first = lax.broadcasted_iota(jnp.int32, (per, group), 0)
    for d in range(n):
        hots[d % 4, d // 4] = (first + d * per == wanted).astype(f32).astype(bf16)
    for k in range(1, planes):
        line_copy(k).wait_recv()
    for k in range(1, 4):
        plane_copy(k).start()
    column = lax.broadcasted_iota(jnp.int32, (group, group * tile), 1)
    owner = lax.broadcasted_iota(jnp.int32, (group, group * tile), 0)
    spread[...] = (column // tile == owner).astype(f32).astype(bf16)
    raw = taps_ref[...]
    weights = (raw / jnp.sum(raw)).astype(bf16)
    tap = lax.broadcasted_iota(jnp.int32, (taps, width), 0)
    lane = lax.broadcasted_iota(jnp.int32, (taps, width), 1)
    place = ((half - tap + width) % width == lane).astype(f32).astype(bf16)
    rows_of[...] = jnp.dot(weights, place, preferred_element_type=f32)
    source = lax.broadcasted_iota(jnp.int32, (width, width), 0)
    target = lax.broadcasted_iota(jnp.int32, (width, width), 1)
    inside = jnp.abs(source - target) <= half
    for a in range(taps):
        line = jnp.broadcast_to(rows_of[a : a + 1, :], (width, width))
        line = pltpu.roll(line, 0, 1, stride=1, stride_axis=0)
        bands[a * width : (a + 1) * width, :] = jnp.where(inside, line, 0.0).astype(bf16)

    picked = jnp.zeros((realizations, group), f32)
    for k in range(4):
        if k:
            plane_copy(k).wait_recv()
        held = lax.rem(q + 4 - k, 4)
        for d in range(planes):
            picked += jnp.dot(slots[held, d], hots[held, d], preferred_element_type=f32)
    repeated = jnp.dot(picked.astype(bf16), spread[...], preferred_element_type=f32)
    inner = lax.broadcasted_iota(jnp.int32, repeated.shape, 1) % tile
    for x in range(tile):
        lhs[x * realizations : (x + 1) * realizations, :] = jnp.where(
            inner == x, repeated, 0.0
        ).astype(bf16)

    def c_copy(step):
        return remote(
            send_c.at[step], recv_c.at[step], c_send.at[step], c_recv.at[step], core_peer
        )

    def y_copy(step):
        return remote(send_y.at[step], recv_y.at[step], y_send.at[step], y_recv.at[step], y_peer)

    def z_copy(step):
        return remote(
            send_z.at[step], recv_z.at[step], z_send.at[step], z_recv.at[step],
            plane_of(step) * 4 + y * 2 + c,
        )

    def multiply(step, across):
        sides = []
        for beside in (0, 1):
            green_copy(step, across, beside).wait()
            sides.append(green[step, across * 2 + beside].reshape(group * tile, width))
        return jnp.dot(lhs[...], jnp.concatenate(sides, axis=1), preferred_element_type=f32)

    def stage(t, carry):
        result = multiply(t, 1)
        for beside in (0, 1):
            send_c[t, beside] = result[:, beside * width : (beside + 1) * width].astype(bf16)
        c_copy(t).start()
        result = multiply(t, 0)
        for beside in (0, 1):
            keep[t, beside] = result[:, beside * width : (beside + 1) * width]

        c_copy(t).wait_recv()
        send_y[t] = (keep[t, 1] + recv_c[t, 1].astype(f32)).astype(bf16)
        y_copy(t).start()
        keep[t, 0] = keep[t, 0] + recv_c[t, 0].astype(f32)

        @pl.when(t >= 1)
        def _():
            step = t - 1
            y_copy(step).wait_recv()
            send_z[step] = (keep[step, 0] + recv_y[step].astype(f32)).astype(bf16)
            z_copy(step).start()

        return carry

    lax.fori_loop(0, planes, stage, 0)
    last = planes - 1
    y_copy(last).wait_recv()
    total = keep[last, 0] + recv_y[last].astype(f32)
    for step in range(last):
        z_copy(step).wait_recv()
        total += recv_z[step].astype(f32)
    padded[edge : edge + rows, :] = total.astype(bf16)

    up = remote(
        padded.at[pl.ds(rows, edge)], padded.at[pl.ds(0, edge)],
        halo_send.at[0], halo_recv.at[0], lax.rem(me + 1, n),
    )
    down = remote(
        padded.at[pl.ds(edge, edge)], padded.at[pl.ds(edge + rows, edge)],
        halo_send.at[1], halo_recv.at[1], lax.rem(me + n - 1, n),
    )
    has_low, has_high = me > 0, me < n - 1
    pl.when(has_high)(lambda: up.start())
    pl.when(has_low)(lambda: down.start())

    @pl.when(me == 0)
    def _():
        padded[0:edge, :] = jnp.zeros((edge, width), bf16)

    @pl.when(me == n - 1)
    def _():
        padded[edge + rows :, :] = jnp.zeros((edge, width), bf16)

    pl.when(has_low)(lambda: up.wait_recv())
    pl.when(has_high)(lambda: down.wait_recv())

    smooth = None
    for begin in range(0, taps, SPAN):
        end = min(taps, begin + SPAN)
        windows = jnp.concatenate(
            [
                padded[a * realizations : a * realizations + rows, :]
                for a in range(begin, end)
            ],
            axis=1,
        )
        term = jnp.dot(
            windows, bands[begin * width : end * width, :], preferred_element_type=f32
        )
        smooth = term if smooth is None else smooth + term
    wet = wet_ref[...].astype(f32)
    for x in range(tile):
        out_ref[x] = smooth[x * realizations : (x + 1) * realizations, :] * wet[x : x + 1, :]

    for k in range(1, planes):
        line_copy(k).wait_send()
    for k in range(1, 4):
        plane_copy(k).wait_send()
    for step in range(planes):
        c_copy(step).wait_send()
        y_copy(step).wait_send()
    for step in range(last):
        z_copy(step).wait_send()
    pl.when(has_high)(lambda: up.wait_send())
    pl.when(has_low)(lambda: down.wait_send())


def on_device(coefficients, kl_modes, green, sub_index, kernel, wet_mask):
    bf16, f32 = jnp.bfloat16, jnp.float32
    n = lax.axis_size("space")
    planes = n // 4
    realizations, modes = coefficients.shape
    per = kl_modes.shape[1]
    group, _, width = green.shape
    tile = wet_mask.shape[0]
    taps = kernel.shape[0]
    rows = tile * realizations
    edge = taps // 2 * realizations
    dma = pltpu.SemaphoreType.DMA
    vmem = pl.BlockSpec(memory_space=pltpu.VMEM)
    hbm = pl.BlockSpec(memory_space=pl.ANY)
    surface = pl.pallas_call(
        functools.partial(source_kernel, n),
        out_shape=jax.ShapeDtypeStruct((tile, realizations, width), f32),
        in_specs=[hbm, hbm, hbm, vmem, vmem, vmem],
        out_specs=vmem,
        scratch_shapes=[
            pltpu.VMEM((realizations, modes), bf16),
            pltpu.VMEM((modes, per), bf16),
            pltpu.VMEM((planes, 4, group, tile, width), bf16),
            pltpu.VMEM((4, planes, realizations, per), bf16),
            pltpu.VMEM((4, planes, per, group), bf16),
            pltpu.VMEM((group, group * tile), bf16),
            pltpu.VMEM((rows, group * tile), bf16),
            pltpu.VMEM((taps * width, width), bf16),
            pltpu.VMEM((taps, width), f32),
            pltpu.VMEM((planes, 2, rows, width), bf16),
            pltpu.VMEM((planes, 2, rows, width), bf16),
            pltpu.VMEM((planes, 2, rows, width), f32),
            pltpu.VMEM((planes, rows, width), bf16),
            pltpu.VMEM((planes, rows, width), bf16),
            pltpu.VMEM((planes, rows, width), bf16),
            pltpu.VMEM((planes, rows, width), bf16),
            pltpu.VMEM((rows + 2 * edge, width), bf16),
            dma((2,)),
            dma((planes, 4)),
            dma((planes + 4,)),
            dma((planes + 4,)),
            dma((planes,)),
            dma((planes,)),
            dma((planes,)),
            dma((planes,)),
            dma((planes,)),
            dma((planes,)),
            dma((2,)),
            dma((2,)),
        ],
        compiler_params=pltpu.CompilerParams(
            collective_id=0, has_side_effects=True, vmem_limit_bytes=56 * 2**20
        ),
    )(coefficients, kl_modes, green, sub_index.reshape(n, group), kernel, wet_mask)
    return surface.transpose(1, 0, 2)


def solution(mesh):
    placed = (
        P("parts", None),
        P("parts", "space"),
        P(("parts", "space"), None, None),
        P("parts"),
        P(),
        P(("parts", "space"), None),
    )
    return jax.shard_map(
        on_device, mesh=mesh, in_specs=placed, out_specs=P("parts", "space", None), check_vma=False
    )
```

```python
import functools
import jax
import jax.numpy as jnp
from jax import lax
from jax.experimental import pallas as pl
from jax.experimental.pallas import tpu as pltpu
from jax.sharding import PartitionSpec as P

SPAN = 8


def remote(source, target, send, receive, peer):
    return pltpu.make_async_remote_copy(
        src_ref=source,
        dst_ref=target,
        send_sem=send,
        recv_sem=receive,
        device_id={"space": peer},
        device_id_type=pl.DeviceIdType.MESH,
    )


def source_kernel(
    n,
    coef_hbm, modes_hbm, green_hbm, index_ref, taps_ref, wet_ref,
    out_ref,
    coef, modes, green, slots, hots, spread, lhs, bands, rows_of,
    send_c, recv_c, keep, send_y, recv_y, send_z, recv_z, padded,
    load_sem, green_sem, slip_send, slip_recv,
    c_send, c_recv, y_send, y_recv, z_send, z_recv, halo_send, halo_recv,
):
    f32, bf16 = jnp.float32, jnp.bfloat16
    me = lax.axis_index("space")
    planes = n // 4
    z, y, c = me // 4, (me // 2) % 2, me % 2
    core_peer = me + 1 - 2 * c
    y_peer = me + 2 - 4 * y
    q = me % 4
    realizations, per = slots.shape[2], slots.shape[3]
    group, tile, width = green.shape[2], green.shape[3], green.shape[4]
    rows = tile * realizations
    taps = taps_ref.shape[0]
    half = taps // 2
    edge = half * realizations

    load_coef = pltpu.make_async_copy(coef_hbm, coef, load_sem.at[0])
    load_modes = pltpu.make_async_copy(modes_hbm, modes, load_sem.at[1])
    load_coef.start()
    load_modes.start()

    def plane_of(step):
        middle = planes // 2
        ahead = jnp.where(step == 0, middle, jnp.where(step < middle, step, step + 1))
        return lax.rem(z + ahead, planes)

    def green_copy(step, across, beside):
        block = plane_of(step) * 4 + ((y + beside) % 2) * 2 + (c + across) % 2
        return pltpu.make_async_copy(
            green_hbm.at[:, pl.ds(pl.multiple_of(block * tile, tile), tile), :],
            green.at[step, across * 2 + beside],
            green_sem.at[step, across * 2 + beside],
        )

    barrier = pltpu.get_barrier_semaphore()
    for k in range(1, n):
        pl.semaphore_signal(
            barrier, inc=1, device_id={"space": lax.rem(me + k, n)},
            device_id_type=pl.DeviceIdType.MESH,
        )
    for step in range(planes):
        for across in (1, 0):
            for beside in (0, 1):
                green_copy(step, across, beside).start()

    load_coef.wait()
    load_modes.wait()
    field = jnp.dot(coef[...], modes[...], preferred_element_type=f32)
    slots[q, z] = jnp.exp(0.5 * field).astype(bf16)
    pl.semaphore_wait(barrier, n - 1)

    def line_copy(k):
        return remote(
            slots.at[q, z], slots.at[q, z], slip_send.at[k], slip_recv.at[k],
            lax.rem(z + k, planes) * 4 + q,
        )

    def plane_copy(k):
        return remote(
            slots.at[q], slots.at[q], slip_send.at[planes + k], slip_recv.at[planes + k],
            z * 4 + lax.rem(q + k, 4),
        )

    for k in range(1, planes):
        line_copy(k).start()

    wanted = index_ref[pl.ds(me, 1), :]
    first = lax.broadcasted_iota(jnp.int32, (per, group), 0)
    for d in range(n):
        hots[d % 4, d // 4] = (first + d * per == wanted).astype(f32).astype(bf16)
    for k in range(1, planes):
        line_copy(k).wait_recv()
    for k in range(1, 4):
        plane_copy(k).start()
    column = lax.broadcasted_iota(jnp.int32, (group, group * tile), 1)
    owner = lax.broadcasted_iota(jnp.int32, (group, group * tile), 0)
    spread[...] = (column // tile == owner).astype(f32).astype(bf16)
    raw = taps_ref[...]
    weights = (raw / jnp.sum(raw)).astype(bf16)
    tap = lax.broadcasted_iota(jnp.int32, (taps, width), 0)
    lane = lax.broadcasted_iota(jnp.int32, (taps, width), 1)
    place = ((half - tap + width) % width == lane).astype(f32).astype(bf16)
    rows_of[...] = jnp.dot(weights, place, preferred_element_type=f32)
    source = lax.broadcasted_iota(jnp.int32, (width, width), 0)
    target = lax.broadcasted_iota(jnp.int32, (width, width), 1)
    inside = jnp.abs(source - target) <= half
    for a in range(taps):
        line = jnp.broadcast_to(rows_of[a : a + 1, :], (width, width))
        line = pltpu.roll(line, 0, 1, stride=1, stride_axis=0)
        bands[a * width : (a + 1) * width, :] = jnp.where(inside, line, 0.0).astype(bf16)

    picked = jnp.zeros((realizations, group), f32)
    for k in range(4):
        if k:
            plane_copy(k).wait_recv()
        held = lax.rem(q + 4 - k, 4)
        for d in range(planes):
            picked += jnp.dot(slots[held, d], hots[held, d], preferred_element_type=f32)
    repeated = jnp.dot(picked.astype(bf16), spread[...], preferred_element_type=f32)
    inner = lax.broadcasted_iota(jnp.int32, repeated.shape, 1) % tile
    for x in range(tile):
        lhs[x * realizations : (x + 1) * realizations, :] = jnp.where(
            inner == x, repeated, 0.0
        ).astype(bf16)

    def c_copy(step):
        return remote(
            send_c.at[step], recv_c.at[step], c_send.at[step], c_recv.at[step], core_peer
        )

    def y_copy(step):
        return remote(send_y.at[step], recv_y.at[step], y_send.at[step], y_recv.at[step], y_peer)

    def z_copy(step):
        return remote(
            send_z.at[step], recv_z.at[step], z_send.at[step], z_recv.at[step],
            plane_of(step) * 4 + y * 2 + c,
        )

    def multiply(step, across):
        sides = []
        for beside in (0, 1):
            green_copy(step, across, beside).wait()
            sides.append(green[step, across * 2 + beside].reshape(group * tile, width))
        return jnp.dot(lhs[...], jnp.concatenate(sides, axis=1), preferred_element_type=f32)

    def stage(t, carry):
        result = multiply(t, 1)
        for beside in (0, 1):
            send_c[t, beside] = result[:, beside * width : (beside + 1) * width].astype(bf16)
        c_copy(t).start()
        result = multiply(t, 0)
        for beside in (0, 1):
            keep[t, beside] = result[:, beside * width : (beside + 1) * width]

        @pl.when(t >= 1)
        def _():
            step = t - 1
            y_copy(step).wait_recv()
            send_z[step] = (keep[step, 0] + recv_y[step].astype(f32)).astype(bf16)
            z_copy(step).start()

        c_copy(t).wait_recv()
        send_y[t] = (keep[t, 1] + recv_c[t, 1].astype(f32)).astype(bf16)
        y_copy(t).start()
        keep[t, 0] = keep[t, 0] + recv_c[t, 0].astype(f32)

        return carry

    lax.fori_loop(0, planes, stage, 0)
    last = planes - 1
    y_copy(last).wait_recv()
    total = keep[last, 0] + recv_y[last].astype(f32)
    for step in range(last):
        z_copy(step).wait_recv()
        total += recv_z[step].astype(f32)
    padded[edge : edge + rows, :] = total.astype(bf16)

    up = remote(
        padded.at[pl.ds(rows, edge)], padded.at[pl.ds(0, edge)],
        halo_send.at[0], halo_recv.at[0], lax.rem(me + 1, n),
    )
    down = remote(
        padded.at[pl.ds(edge, edge)], padded.at[pl.ds(edge + rows, edge)],
        halo_send.at[1], halo_recv.at[1], lax.rem(me + n - 1, n),
    )
    has_low, has_high = me > 0, me < n - 1
    pl.when(has_high)(lambda: up.start())
    pl.when(has_low)(lambda: down.start())

    @pl.when(me == 0)
    def _():
        padded[0:edge, :] = jnp.zeros((edge, width), bf16)

    @pl.when(me == n - 1)
    def _():
        padded[edge + rows :, :] = jnp.zeros((edge, width), bf16)

    pl.when(has_low)(lambda: up.wait_recv())
    pl.when(has_high)(lambda: down.wait_recv())

    smooth = None
    for begin in range(0, taps, SPAN):
        end = min(taps, begin + SPAN)
        windows = jnp.concatenate(
            [
                padded[a * realizations : a * realizations + rows, :]
                for a in range(begin, end)
            ],
            axis=1,
        )
        term = jnp.dot(
            windows, bands[begin * width : end * width, :], preferred_element_type=f32
        )
        smooth = term if smooth is None else smooth + term
    wet = wet_ref[...].astype(f32)
    for x in range(tile):
        out_ref[x] = smooth[x * realizations : (x + 1) * realizations, :] * wet[x : x + 1, :]

    for k in range(1, planes):
        line_copy(k).wait_send()
    for k in range(1, 4):
        plane_copy(k).wait_send()
    for step in range(planes):
        c_copy(step).wait_send()
        y_copy(step).wait_send()
    for step in range(last):
        z_copy(step).wait_send()
    pl.when(has_high)(lambda: up.wait_send())
    pl.when(has_low)(lambda: down.wait_send())


def on_device(coefficients, kl_modes, green, sub_index, kernel, wet_mask):
    bf16, f32 = jnp.bfloat16, jnp.float32
    n = lax.axis_size("space")
    planes = n // 4
    realizations, modes = coefficients.shape
    per = kl_modes.shape[1]
    group, _, width = green.shape
    tile = wet_mask.shape[0]
    taps = kernel.shape[0]
    rows = tile * realizations
    edge = taps // 2 * realizations
    dma = pltpu.SemaphoreType.DMA
    vmem = pl.BlockSpec(memory_space=pltpu.VMEM)
    hbm = pl.BlockSpec(memory_space=pl.ANY)
    surface = pl.pallas_call(
        functools.partial(source_kernel, n),
        out_shape=jax.ShapeDtypeStruct((tile, realizations, width), f32),
        in_specs=[hbm, hbm, hbm, vmem, vmem, vmem],
        out_specs=vmem,
        scratch_shapes=[
            pltpu.VMEM((realizations, modes), bf16),
            pltpu.VMEM((modes, per), bf16),
            pltpu.VMEM((planes, 4, group, tile, width), bf16),
            pltpu.VMEM((4, planes, realizations, per), bf16),
            pltpu.VMEM((4, planes, per, group), bf16),
            pltpu.VMEM((group, group * tile), bf16),
            pltpu.VMEM((rows, group * tile), bf16),
            pltpu.VMEM((taps * width, width), bf16),
            pltpu.VMEM((taps, width), f32),
            pltpu.VMEM((planes, 2, rows, width), bf16),
            pltpu.VMEM((planes, 2, rows, width), bf16),
            pltpu.VMEM((planes, 2, rows, width), f32),
            pltpu.VMEM((planes, rows, width), bf16),
            pltpu.VMEM((planes, rows, width), bf16),
            pltpu.VMEM((planes, rows, width), bf16),
            pltpu.VMEM((planes, rows, width), bf16),
            pltpu.VMEM((rows + 2 * edge, width), bf16),
            dma((2,)),
            dma((planes, 4)),
            dma((planes + 4,)),
            dma((planes + 4,)),
            dma((planes,)),
            dma((planes,)),
            dma((planes,)),
            dma((planes,)),
            dma((planes,)),
            dma((planes,)),
            dma((2,)),
            dma((2,)),
        ],
        compiler_params=pltpu.CompilerParams(
            collective_id=0, has_side_effects=True, vmem_limit_bytes=56 * 2**20
        ),
    )(coefficients, kl_modes, green, sub_index.reshape(n, group), kernel, wet_mask)
    return surface.transpose(1, 0, 2)


def solution(mesh):
    placed = (
        P("parts", None),
        P("parts", "space"),
        P(("parts", "space"), None, None),
        P("parts"),
        P(),
        P(("parts", "space"), None),
    )
    return jax.shard_map(
        on_device, mesh=mesh, in_specs=placed, out_specs=P("parts", "space", None), check_vma=False
    )
```
